128 devices in a mesh: ctx: 32 (over y, z, core), uly: 4 (over x).
Axes of the slice: x: 4, y: 4, z: 4, core: 2. Of those that a mesh axis runs over, the one named last changes fastest.
Arguments:
- queries: bfloat16 [24576, 4096], P(('ctx', 'uly')), may hold values from -24 to 24
- keys: bfloat16 [24576, 4096], P(('ctx', 'uly')), may hold values from -6 to 6
- values: bfloat16 [24576, 4096], P(('ctx', 'uly')), may hold values from -6 to 6
- d_out: bfloat16 [24576, 4096], P(('ctx', 'uly')), may hold values from -6 to 6
- doc_lengths: int32 [64], replicated, may hold values from 1 to 768, 24576 in all
Outputs:
- attn_out: bfloat16 [24576, 4096], P(('ctx', 'uly'))
- d_queries: bfloat16 [24576, 4096], P(('ctx', 'uly'))
- d_keys: bfloat16 [24576, 4096], P(('ctx', 'uly'))
- d_values: bfloat16 [24576, 4096], P(('ctx', 'uly'))
The draws below stay inside these ranges and needn't reach their ends.
Inputs may be any that keep to these rules, and one draw needn't show every extreme that they name: `doc_lengths`: the lengths sum to 24576.
All inputs are finite; a program needn't handle non-finite values.
Results may differ from the reference program's by a relative error of at most 0.012.
The reference program's roundings to bfloat16 on the way count: a program that leaves them out, or rounds other values in their place, can miss the bound.
Values may be sent and summed in bfloat16 or wider, within the bound.
No kernel may reach another device: no remote copies, remote signals or barrier semaphores. Data moves between devices by JAX's collectives and lax.ppermute only.
A program may use at most 192 MiB of HBM per device.

```python
import math
import jax
import jax.numpy as jnp
import numpy as np
from jax import lax

HEADS = 32
HEAD_DIM = 128
TOK_DEV = 192
REACH = 1
TOKENS = 24576
DOC_MOST = 768
NDOCS = 64
N_CTX = 32
N_ULY = 4


def draw_queries(key, part):
    key = jax.random.fold_in(key, 3)
    drawn = jnp.clip(jax.random.normal(key, (TOKENS, HEADS * HEAD_DIM)), -6.0, 6.0)
    return drawn.astype(jnp.bfloat16)


def draw_keys(key, part):
    key = jax.random.fold_in(key, 5)
    drawn = jnp.clip(jax.random.normal(key, (TOKENS, HEADS * HEAD_DIM)), -6.0, 6.0)
    return drawn.astype(jnp.bfloat16)


def block_levels(key, extent, shards, least, top_value):
    def one(dim, shards_of):
        draws = jax.random.uniform(jax.random.fold_in(jax.random.fold_in(key, 6), dim), (shards_of,), jnp.float32, least / len(shards), top_value / len(shards))
        return jnp.repeat(jnp.exp(draws), extent[dim] // shards_of).reshape((-1,) + (1,) * (len(extent) - dim - 1))

    loudness = one(*shards[0])
    for cut in shards[1:]:
        loudness = loudness * one(*cut)
    return loudness


def length_profile(amount, total, most, skew):
    portions = [(1 << 20) // math.isqrt(rank ** skew) + 1 for rank in range(2, amount + 1)]
    surplus, counts = total - most - (amount - 1), [1] * (amount - 1)
    while surplus > 0:
        movable = [i for i in range(amount - 1) if counts[i] < most]
        pool, left = sum([portions[i] for i in movable]), surplus
        for i in movable:
            extra = min(most - counts[i], max(1, left * portions[i] // pool), surplus)
            counts[i] = counts[i] + extra
            surplus = surplus - extra
    return np.array([most] + counts)


def uneven(rng, number_of, total, limit, slope):
    if number_of == 2:
        one = jax.random.randint(rng, (), max(1, total - limit), min(limit, total - 1) + 1)
        return jnp.stack([one, total - one])
    tallies = jnp.asarray(length_profile(number_of, total, limit, slope), jnp.int32)
    couples = (number_of - 1) // 2
    donor, sink = tallies[1:1 + 2 * couples:2], tallies[2:2 + 2 * couples:2]
    room = jnp.minimum(donor - 1, limit - sink)
    passed = jax.random.randint(jax.random.fold_in(rng, 1), (couples,), 0, 1 << 20) % (room + 1)
    tallies = tallies.at[1:1 + 2 * couples:2].set(donor - passed).at[2:2 + 2 * couples:2].set(sink + passed)
    return tallies[jax.random.permutation(jax.random.fold_in(rng, 2), number_of)]


def bell_draw(key, extent, scale, bound, pieces=(), kind=jnp.bfloat16):
    values = jax.random.normal(key, extent, jnp.float32) * scale
    if len(pieces) > 0:
        values = block_levels(key, extent, pieces, -0.22, 0.18) * values
    return jnp.clip(values, min=-bound, max=bound).astype(kind)


def setup_inputs(seed: int = 0) -> dict:
    splits = jax.random.split(jax.random.key(seed), 6)
    return {
        "queries": draw_queries(jax.random.fold_in(splits[5], 71), 0),
        "keys": draw_keys(jax.random.fold_in(splits[5], 71), 0),
        "values": bell_draw(splits[2], (TOKENS, HEADS * HEAD_DIM), 1.0, 6.0, ((0, 128),)),
        "d_out": bell_draw(splits[3], (TOKENS, HEADS * HEAD_DIM), 1.0, 6.0, ((0, 128),)),
        "doc_lengths": uneven(splits[4], NDOCS, TOKENS, DOC_MOST, 2).astype(jnp.int32),
    }


masked_score = -1.0e30


def doc_index(positions, doc_ends):
    inside = jnp.sum((doc_ends[None, :] <= positions[:, None]).astype(jnp.int32), axis=1)
    return jnp.where(positions < 0, -1, inside).astype(jnp.int32)


def reference(queries, keys, values, d_out, doc_lengths):
    doc_ends = jnp.cumsum(doc_lengths).astype(jnp.int32)
    block_rows = TOK_DEV * N_ULY
    margin = REACH * block_rows
    window = block_rows + 2 * margin
    score_scale = HEAD_DIM ** -0.5
    block_iota = jnp.arange(block_rows, dtype=jnp.int32)
    window_iota = jnp.arange(window, dtype=jnp.int32)

    def padded(array):
        return jnp.pad(array, ((margin, margin), (0, 0))).reshape(TOKENS + 2 * margin, HEADS, HEAD_DIM)

    query_pad = padded(queries)
    key_pad = padded(keys)
    value_pad = padded(values)
    grad_pad = padded(d_out)

    def query_block(block_index):
        first_row = (block_index * block_rows).astype(jnp.int32)
        query_blk = lax.dynamic_slice_in_dim(query_pad, first_row + margin, block_rows, 0).astype(jnp.float32)
        grad_blk = lax.dynamic_slice_in_dim(grad_pad, first_row + margin, block_rows, 0).astype(jnp.float32)
        key_win = lax.dynamic_slice_in_dim(key_pad, first_row, window, 0).astype(jnp.float32)
        value_win = lax.dynamic_slice_in_dim(value_pad, first_row, window, 0).astype(jnp.float32)
        same_doc = doc_index(first_row + block_iota, doc_ends)[:, None] == doc_index(first_row - margin + window_iota, doc_ends)[None, :]
        scores = jnp.where(same_doc[None], score_scale * jnp.einsum("qhe,khe->hqk", query_blk, key_win), masked_score)
        row_max = jnp.max(scores, axis=2, keepdims=True)
        log_total = row_max + jnp.log(jnp.sum(jnp.exp(scores - row_max), axis=2, keepdims=True))
        weights = jnp.exp(scores - log_total).astype(jnp.bfloat16)
        weights_wide = lax.optimization_barrier(weights).astype(jnp.float32)
        out_blk = jnp.einsum("hqk,khe->qhe", weights_wide, value_win).astype(jnp.bfloat16)
        out_wide = lax.optimization_barrier(out_blk).astype(jnp.float32)
        row_delta = jnp.sum(grad_blk * out_wide, axis=2)
        grad_scores = (weights_wide * (jnp.einsum("qhe,khe->hqk", grad_blk, value_win) - row_delta.T[:, :, None])).astype(jnp.bfloat16)
        grad_wide = lax.optimization_barrier(grad_scores).astype(jnp.float32)
        dq_blk = (score_scale * jnp.einsum("hqk,khe->qhe", grad_wide, key_win)).astype(jnp.bfloat16)
        return out_blk, dq_blk, log_total[:, :, 0].T, row_delta

    out_all, dq_all, total_all, delta_all = lax.map(query_block, jnp.arange(N_CTX, dtype=jnp.int32))
    total_pad = jnp.pad(total_all.reshape(TOKENS, HEADS), ((margin, margin), (0, 0)))
    delta_pad = jnp.pad(delta_all.reshape(TOKENS, HEADS), ((margin, margin), (0, 0)))

    def key_block(block_index):
        first_row = (block_index * block_rows).astype(jnp.int32)
        key_blk = lax.dynamic_slice_in_dim(key_pad, first_row + margin, block_rows, 0).astype(jnp.float32)
        value_blk = lax.dynamic_slice_in_dim(value_pad, first_row + margin, block_rows, 0).astype(jnp.float32)
        query_win = lax.dynamic_slice_in_dim(query_pad, first_row, window, 0).astype(jnp.float32)
        grad_win = lax.dynamic_slice_in_dim(grad_pad, first_row, window, 0).astype(jnp.float32)
        total_win = lax.dynamic_slice_in_dim(total_pad, first_row, window, 0)
        delta_win = lax.dynamic_slice_in_dim(delta_pad, first_row, window, 0)
        same_doc = doc_index(first_row - margin + window_iota, doc_ends)[:, None] == doc_index(first_row + block_iota, doc_ends)[None, :]
        scores = jnp.where(same_doc[None], score_scale * jnp.einsum("qhe,khe->hqk", query_win, key_blk), masked_score)
        weights = jnp.exp(scores - total_win.T[:, :, None]).astype(jnp.bfloat16)
        weights_wide = lax.optimization_barrier(weights).astype(jnp.float32)
        dv_blk = jnp.einsum("hqk,qhe->khe", weights_wide, grad_win).astype(jnp.bfloat16)
        grad_scores = (weights_wide * (jnp.einsum("qhe,khe->hqk", grad_win, value_blk) - delta_win.T[:, :, None])).astype(jnp.bfloat16)
        grad_wide = lax.optimization_barrier(grad_scores).astype(jnp.float32)
        dk_blk = (score_scale * jnp.einsum("hqk,qhe->khe", grad_wide, query_win)).astype(jnp.bfloat16)
        return dk_blk, dv_blk

    dk_all, dv_all = lax.map(key_block, jnp.arange(N_CTX, dtype=jnp.int32))
    shape = (TOKENS, HEADS * HEAD_DIM)
    return out_all.reshape(shape), dq_all.reshape(shape), dk_all.reshape(shape), dv_all.reshape(shape)
```

```python
import jax
import jax.numpy as jnp
from jax import lax
from jax.sharding import PartitionSpec as P

HEAD_DIM = 128


masked_score = -1e30


def shifted(value, axis, by):
    count = lax.axis_size(axis)
    pairs = [(i, i + by) for i in range(count) if 0 <= i + by < count]
    return lax.ppermute(value, axis, pairs)


def doc_index(positions, doc_ends):
    inside = jnp.sum((doc_ends[None, :] <= positions[:, None]).astype(jnp.int32), axis=1)
    return jnp.where(positions < 0, -1, inside)


def contract_last(left, right):
    return lax.dot_general(
        left, right, (((1,), (1,)), ((), ())), preferred_element_type=jnp.float32
    )


def contract_first(left, right):
    return lax.dot_general(
        left, right, (((0,), (0,)), ((), ())), preferred_element_type=jnp.float32
    )


def head_slice(array, column):
    return lax.dynamic_slice_in_dim(array, column, HEAD_DIM, 1)


def on_device(queries, keys, values, d_out, doc_lengths):
    query_loc, key_loc, value_loc, grad_loc = (
        lax.all_to_all(queries, "uly", split_axis=1, concat_axis=0, tiled=True),
        lax.all_to_all(keys, "uly", split_axis=1, concat_axis=0, tiled=True),
        lax.all_to_all(values, "uly", split_axis=1, concat_axis=0, tiled=True),
        lax.all_to_all(d_out, "uly", split_axis=1, concat_axis=0, tiled=True),
    )
    row_count = query_loc.shape[0]
    columns = query_loc.shape[1]
    heads_here = columns // HEAD_DIM
    score_scale = HEAD_DIM ** (-0.5)
    doc_iota = jnp.arange(doc_lengths.shape[0], dtype=jnp.int32)
    doc_ends = jnp.sum(
        jnp.where(doc_iota[None, :] <= doc_iota[:, None], doc_lengths[None, :], 0), axis=1
    )
    shard_index = lax.axis_index("ctx")
    offsets = []
    offsets = offsets + [1, -1]
    row_iota = jnp.arange(row_count, dtype=jnp.int32)
    own_docs = doc_index(shard_index * row_count + row_iota, doc_ends)
    key_list = [key_loc]
    value_list = [value_loc]
    doc_list = [own_docs]
    for offset in offsets:
        moved_keys, moved_values = shifted((key_loc, value_loc), "ctx", offset)
        key_list.append(moved_keys)
        value_list.append(moved_values)
        doc_list.append(doc_index((shard_index - offset) * row_count + row_iota, doc_ends))
    key_all = jnp.concatenate(key_list, axis=0)
    value_all = jnp.concatenate(value_list, axis=0)
    near_docs = jnp.concatenate(doc_list, axis=0)
    query_same = own_docs[:, None] == near_docs[None, :]
    near_rows = key_all.shape[0]
    part_shape = (near_rows, columns)

    def query_step(head_index, carry):
        out_acc, dq_acc, stat_total, stat_delta, dk_acc, dv_acc = carry
        column = head_index * HEAD_DIM
        query_head = head_slice(query_loc, column)
        key_head = head_slice(key_all, column)
        value_head = head_slice(value_all, column)
        grad_head = head_slice(grad_loc, column)
        scores = jnp.where(
            query_same, score_scale * contract_last(query_head, key_head), masked_score
        )
        row_max = jnp.max(scores, axis=1, keepdims=True)
        log_total = row_max + jnp.log(jnp.sum(jnp.exp(scores - row_max), axis=1, keepdims=True))
        weights = jnp.exp(scores - log_total).astype(jnp.bfloat16)
        out_head = jnp.dot(weights, value_head, preferred_element_type=jnp.float32).astype(
            jnp.bfloat16
        )
        row_delta = jnp.sum(
            grad_head.astype(jnp.float32) * lax.optimization_barrier(out_head).astype(jnp.float32),
            axis=1,
            keepdims=True,
        )
        grad_scores = (
            lax.optimization_barrier(weights).astype(jnp.float32)
            * (contract_last(grad_head, value_head) - row_delta)
        ).astype(jnp.bfloat16)
        dq_head = (
            score_scale * jnp.dot(grad_scores, key_head, preferred_element_type=jnp.float32)
        ).astype(jnp.bfloat16)
        out_acc = lax.dynamic_update_slice_in_dim(out_acc, out_head, column, 1)
        dq_acc = lax.dynamic_update_slice_in_dim(dq_acc, dq_head, column, 1)
        stat_total = lax.dynamic_update_slice_in_dim(stat_total, log_total, head_index, 1)
        stat_delta = lax.dynamic_update_slice_in_dim(stat_delta, row_delta, head_index, 1)
        dk_acc = lax.dynamic_update_slice_in_dim(
            dk_acc, score_scale * contract_first(grad_scores, query_head), column, 1
        )
        dv_acc = lax.dynamic_update_slice_in_dim(
            dv_acc, contract_first(weights, grad_head), column, 1
        )
        return (out_acc, dq_acc, stat_total, stat_delta, dk_acc, dv_acc)

    start_carry = (
        jnp.zeros((row_count, columns), jnp.bfloat16),
        jnp.zeros((row_count, columns), jnp.bfloat16),
        jnp.zeros((row_count, heads_here), jnp.float32),
        jnp.zeros((row_count, heads_here), jnp.float32),
        jnp.zeros(part_shape, jnp.float32),
        jnp.zeros(part_shape, jnp.float32),
    )
    out_loc, dq_loc, stat_total, stat_delta, dk_acc, dv_acc = lax.fori_loop(
        0, heads_here, query_step, start_carry
    )
    key_sum = dk_acc[:row_count]
    value_sum = dv_acc[:row_count]
    for segment, offset in enumerate(offsets):
        first_row = (segment + 1) * row_count
        back_keys, back_values = shifted(
            (dk_acc[first_row : first_row + row_count], dv_acc[first_row : first_row + row_count]),
            "ctx",
            -offset,
        )
        key_sum = key_sum + back_keys
        value_sum = value_sum + back_values
    dk_loc = key_sum.astype(jnp.bfloat16)
    dv_loc = value_sum.astype(jnp.bfloat16)
    attn_out, d_queries, d_keys, d_values = (
        lax.all_to_all(out_loc, "uly", split_axis=0, concat_axis=1, tiled=True),
        lax.all_to_all(dq_loc, "uly", split_axis=0, concat_axis=1, tiled=True),
        lax.all_to_all(dk_loc, "uly", split_axis=0, concat_axis=1, tiled=True),
        lax.all_to_all(dv_loc, "uly", split_axis=0, concat_axis=1, tiled=True),
    )
    return (attn_out, d_queries, d_keys, d_values)


def solution(mesh):
    return jax.shard_map(
        on_device,
        mesh=mesh,
        in_specs=(
            P(("ctx", "uly"), None),
            P(("ctx", "uly"), None),
            P(("ctx", "uly"), None),
            P(("ctx", "uly"), None),
            P(),
        ),
        out_specs=(
            P(("ctx", "uly"), None),
            P(("ctx", "uly"), None),
            P(("ctx", "uly"), None),
            P(("ctx", "uly"), None),
        ),
        check_vma=False,
    )
```
